32 devices in a mesh: ka: 8 (over y, x, core), pw: 4 (over z).
Axes of the slice: x: 2, y: 2, z: 4, core: 2. Of those that a mesh axis runs over, the one named last changes fastest.
Arguments:
- coeffs: bfloat16 [128, 2, 1536, 256], P('ka', None, 'pw'), may hold values from -2.5 to 2.5
- neighbour: int32 [128], P('ka'), may hold values from 0 to 127, as said below
- gshift: int32 [1536], replicated, may hold values from 0 to 1535, each once
Outputs:
- inner_products: float32 [256, 128, 2, 256], P('pw', 'ka')
The draws below stay inside these ranges and needn't reach their ends.
Inputs may be any that keep to these rules, and one draw needn't show every extreme that they name: neighbour[k] lies in the slab of 16 k-points that starts 2 * 16 points after the start of the slab of k, counted cyclically over the 128 points; the neighbours of one slab's points are distinct. `gshift`: each row appears once.
All inputs are finite; a program needn't handle non-finite values.
Results may differ from the reference program's by a relative error of at most 0.0003.
Values may be sent and summed in bfloat16 or wider, within the bound.
A program may use at most 128 MiB of HBM per device.

```python
import jax
import jax.numpy as jnp
from jax import lax

NB = 256
K_DEV = 16
SHIFT_DEV = 2
K = 128
PW = 1536
N_KA = 8


def draw_neighbour(key, part):
    slab_total = K // K_DEV
    slab_keys = jax.random.split(key, slab_total)
    orders = jax.vmap(lambda single_key: jax.random.permutation(single_key, K_DEV))(slab_keys)
    target = (jnp.arange(slab_total, dtype=jnp.int32) + SHIFT_DEV) % slab_total
    return (target[:, None] * K_DEV + orders.astype(jnp.int32)).reshape(K).astype(jnp.int32)


def block_scale(own_key, dims, cuts, low, top_value):
    def one(position, shards_of):
        steps = jax.random.uniform(jax.random.fold_in(jax.random.fold_in(own_key, 6), position), (shards_of,), jnp.float32, low / len(cuts), top_value / len(cuts))
        return jnp.repeat(jnp.exp(steps), dims[position] // shards_of).reshape((-1,) + (1,) * (len(dims) - position - 1))

    loudness = one(*cuts[0])
    for cut in cuts[1:]:
        loudness = loudness * one(*cut)
    return loudness


def scatter_about(rng, shape, scale, limit, cuts=(), kind=jnp.bfloat16):
    array = scale * jax.random.normal(rng, shape, jnp.float32)
    if cuts:
        array = array * block_scale(rng, shape, cuts, -0.22, 0.18)
    return jnp.clip(array, -limit, limit).astype(kind)


def setup_inputs(seed: int = 0) -> dict:
    streams_of = jax.random.split(jax.random.key(seed), 4)
    return {
        "coeffs": scatter_about(streams_of[0], (K, 2, PW, NB), (PW ** -0.25), 2.5, ((0, 8), (2, 4))),
        "neighbour": draw_neighbour(jax.random.fold_in(streams_of[3], 71), 0),
        "gshift": jax.random.permutation(streams_of[2], PW).astype(jnp.int32),
    }


def pair_single(own_block, partner_block):
    products_all = jnp.einsum("cgm,dgn->cdmn", own_block.astype(jnp.float32), partner_block.astype(jnp.float32), precision=lax.Precision.HIGHEST)
    real_part = products_all[0, 0] + products_all[1, 1]
    imag_part = products_all[0, 1] - products_all[1, 0]
    return jnp.stack([real_part, imag_part], axis=1)


def reference(coeffs, neighbour, gshift):
    def single(point):
        own_block = coeffs[point]
        partner_block = coeffs[neighbour[point]]
        permuted = jnp.take(partner_block, gshift, axis=1)
        wrapped = point // K_DEV >= N_KA - SHIFT_DEV
        partner_block = jnp.where(wrapped, permuted, partner_block)
        return pair_single(own_block, partner_block)

    result = lax.map(single, jnp.arange(K, dtype=jnp.int32))
    return jnp.transpose(result, (1, 0, 2, 3))
```

```python
import functools

import jax
import jax.numpy as jnp
from jax import lax
from jax.experimental import pallas as pl
from jax.experimental.pallas import tpu as pltpu
from jax.sharding import PartitionSpec as P

SHIFT_DEV = 2
GROUP = 2
MESH = pl.DeviceIdType.MESH
SENT = jnp.float32


def contract(a, b):
    return lax.dot_general(a, b, (((0,), (0,)), ((), ())), preferred_element_type=jnp.float32)


def kernel(n_ka, n_pw, inv_ref, gshift_ref, x_ref, out_ref, y, own_k, sorted_own, sent, got, part, moved,
           y_send, y_recv, k_send, k_recv, p_send, p_recv):
    slab, _, rows, bands = x_ref.shape
    per_pw = slab // n_pw
    groups = slab // GROUP
    cut = bands // n_pw
    ka, pw = lax.axis_index("ka"), lax.axis_index("pw")
    source = lax.rem(ka + SHIFT_DEV, n_ka)
    target = lax.rem(ka + n_ka - SHIFT_DEV, n_ka)
    wrapped = ka >= n_ka - SHIFT_DEV
    feeds_wrapped = ka < SHIFT_DEV

    def peer(d):
        return lax.rem(pw + d, n_pw)

    barrier = pltpu.get_barrier_semaphore()

    @pl.loop(1, n_pw)
    def _(d):
        pl.semaphore_signal(barrier, inc=1, device_id=(ka, peer(d)), device_id_type=MESH)

    @pl.when(wrapped)
    def _():
        @pl.loop(0, n_pw)
        def _(d):
            pl.semaphore_signal(barrier, inc=1, device_id=(source, peer(d)), device_id_type=MESH)

    @pl.when(jnp.logical_not(wrapped))
    def _():
        pl.semaphore_signal(barrier, inc=1, device_id=(source, pw), device_id_type=MESH)

    @pl.when(feeds_wrapped)
    def _():
        pl.semaphore_wait(barrier, 2 * n_pw - 1)

    @pl.when(jnp.logical_not(feeds_wrapped))
    def _():
        pl.semaphore_wait(barrier, n_pw)

    def shift_plain(k):
        return pltpu.make_async_remote_copy(
            src_ref=x_ref.at[k], dst_ref=y.at[k], send_sem=y_send.at[k], recv_sem=y_recv.at[k],
            device_id=(target, pw), device_id_type=MESH)

    def shift_to_wrapped(kk, d):
        k = peer(d) * per_pw + kk
        slot = pw * per_pw + kk
        return pltpu.make_async_remote_copy(
            src_ref=x_ref.at[k], dst_ref=y.at[slot], send_sem=y_send.at[k], recv_sem=y_recv.at[slot],
            device_id=(target, peer(d)), device_id_type=MESH)

    def own_to_peer(kk, d):
        k = peer(d) * per_pw + kk
        slot = pw * per_pw + kk
        return pltpu.make_async_remote_copy(
            src_ref=sorted_own.at[k], dst_ref=own_k.at[slot], send_sem=k_send.at[k], recv_sem=k_recv.at[slot],
            device_id=(ka, peer(d)), device_id_type=MESH)

    def part_to_peer(g, d):
        return pltpu.make_async_remote_copy(
            src_ref=sent.at[pl.ds(g * GROUP, GROUP), :, pl.ds(pl.multiple_of(peer(d) * cut, cut), cut), :],
            dst_ref=got.at[pw, pl.ds(g * GROUP, GROUP)],
            send_sem=p_send.at[g, peer(d)], recv_sem=p_recv.at[g, pw],
            device_id=(ka, peer(d)), device_id_type=MESH)

    def part_from_peer(g, d):
        return pltpu.make_async_remote_copy(
            src_ref=sent.at[pl.ds(g * GROUP, GROUP), :, pl.ds(pl.multiple_of(peer(d) * cut, cut), cut), :],
            dst_ref=got.at[peer(d), pl.ds(g * GROUP, GROUP)],
            send_sem=p_send.at[g, peer(d)], recv_sem=p_recv.at[g, peer(d)],
            device_id=(ka, peer(d)), device_id_type=MESH)

    def whole_to_peer(kk, d):
        k = pw * per_pw + kk
        return pltpu.make_async_remote_copy(
            src_ref=sent.at[k, :, pl.ds(pl.multiple_of(peer(d) * cut, cut), cut), :],
            dst_ref=got.at[pw, k],
            send_sem=p_send.at[kk, peer(d)], recv_sem=p_recv.at[kk, pw],
            device_id=(ka, peer(d)), device_id_type=MESH)

    def whole_from_peer(kk, d):
        k = peer(d) * per_pw + kk
        return pltpu.make_async_remote_copy(
            src_ref=sent.at[k, :, pl.ds(pl.multiple_of(peer(d) * cut, cut), cut), :],
            dst_ref=got.at[peer(d), k],
            send_sem=p_send.at[kk, peer(d)], recv_sem=p_recv.at[kk, peer(d)],
            device_id=(ka, peer(d)), device_id_type=MESH)

    @pl.when(feeds_wrapped)
    def _():
        @pl.loop(0, per_pw)
        def _(kk):
            @pl.loop(0, n_pw)
            def _(d):
                shift_to_wrapped(kk, d).start()

    @pl.when(jnp.logical_not(feeds_wrapped))
    def _():
        @pl.loop(0, slab)
        def _(k):
            shift_plain(k).start()

    def keep(k):
        sent[k] = part[...].astype(SENT)
        out_ref[k] = part[:, pl.ds(pl.multiple_of(pw * cut, cut), cut), :]

    @pl.when(jnp.logical_not(wrapped))
    def _():
        @pl.loop(0, groups)
        def _(g):
            @pl.loop(0, GROUP)
            def _(kk):
                k = g * GROUP + kk
                pltpu.make_async_remote_copy(
                    src_ref=x_ref.at[k], dst_ref=y.at[k], send_sem=y_send.at[k], recv_sem=y_recv.at[k],
                    device_id=(target, pw), device_id_type=MESH).wait_recv()
                mine = x_ref[inv_ref[k]]
                other = y[k]
                part[0] = contract(mine.reshape(2 * rows, bands), other.reshape(2 * rows, bands))
                part[1] = contract(mine[0], other[1]) - contract(mine[1], other[0])
                keep(k)

            @pl.loop(1, n_pw)
            def _(d):
                part_to_peer(g, d).start()

        @pl.loop(0, groups)
        def _(g):
            @pl.loop(1, n_pw)
            def _(d):
                part_from_peer(g, d).wait_recv()
                span = pl.ds(g * GROUP, GROUP)
                out_ref[span] = out_ref[span] + got[peer(d), span].astype(jnp.float32)

        @pl.loop(0, groups)
        def _(g):
            @pl.loop(1, n_pw)
            def _(d):
                part_to_peer(g, d).wait_send()

    @pl.when(wrapped)
    def _():
        @pl.loop(0, per_pw)
        def _(kk):
            own_k[pw * per_pw + kk] = x_ref[inv_ref[pw * per_pw + kk]]

            @pl.loop(1, n_pw)
            def _(d):
                k = peer(d) * per_pw + kk
                sorted_own[k] = x_ref[inv_ref[k]]
                own_to_peer(kk, d).start()

        @pl.loop(0, per_pw)
        def _(kk):
            @pl.loop(0, n_pw)
            def _(s):
                slot = s * per_pw + kk
                pltpu.make_async_remote_copy(
                    src_ref=x_ref.at[slot], dst_ref=y.at[slot], send_sem=y_send.at[slot], recv_sem=y_recv.at[slot],
                    device_id=(target, pw), device_id_type=MESH).wait_recv()

            @pl.loop(1, n_pw)
            def _(d):
                slot = peer(d) * per_pw + kk
                pltpu.make_async_remote_copy(
                    src_ref=sorted_own.at[slot], dst_ref=own_k.at[slot], send_sem=k_send.at[slot],
                    recv_sem=k_recv.at[slot], device_id=(ka, peer(d)), device_id_type=MESH).wait_recv()

            part[...] = jnp.zeros_like(part)

            @pl.loop(0, n_pw)
            def _(i):
                wanted = gshift_ref[pl.ds(pl.multiple_of(i * rows, rows), rows), :]
                moved[...] = jnp.zeros_like(moved)

                @pl.loop(0, n_pw)
                def _(s):
                    place = lax.broadcasted_iota(jnp.int32, (rows, rows), 1) + s * rows
                    chosen = jnp.where(place == wanted, 1.0, 0.0).astype(jnp.bfloat16)
                    for c in range(2):
                        moved[c] += jnp.dot(chosen, y[s * per_pw + kk, c], preferred_element_type=jnp.float32)

                mine = own_k[i * per_pw + kk]
                other = moved[...].astype(jnp.bfloat16)
                part[0] += contract(mine.reshape(2 * rows, bands), other.reshape(2 * rows, bands))
                part[1] += contract(mine[0], other[1]) - contract(mine[1], other[0])

            keep(pw * per_pw + kk)

            @pl.loop(1, n_pw)
            def _(d):
                whole_to_peer(kk, d).start()

        @pl.loop(0, per_pw)
        def _(kk):
            @pl.loop(1, n_pw)
            def _(d):
                whole_from_peer(kk, d).wait_recv()
                k = peer(d) * per_pw + kk
                out_ref[k] = got[peer(d), k].astype(jnp.float32)

        @pl.loop(0, per_pw)
        def _(kk):
            @pl.loop(1, n_pw)
            def _(d):
                whole_to_peer(kk, d).wait_send()
                own_to_peer(kk, d).wait_send()

    @pl.when(feeds_wrapped)
    def _():
        @pl.loop(0, per_pw)
        def _(kk):
            @pl.loop(0, n_pw)
            def _(d):
                shift_to_wrapped(kk, d).wait_send()

    @pl.when(jnp.logical_not(feeds_wrapped))
    def _():
        @pl.loop(0, slab)
        def _(k):
            shift_plain(k).wait_send()


def on_device(n_ka, n_pw, coeffs, neighbour, gshift):
    slab, parts, rows, bands = coeffs.shape
    cut = bands // n_pw
    points = jnp.arange(slab, dtype=jnp.int32)
    local_order = neighbour % slab
    inverse = jnp.sum(jnp.where(local_order[:, None] == points[None, :], points[:, None], 0), axis=0)
    vmem = pl.BlockSpec(memory_space=pltpu.VMEM)
    flops = 8 * slab * rows * bands * bands
    summed = pl.pallas_call(
        functools.partial(kernel, n_ka, n_pw),
        out_shape=jax.ShapeDtypeStruct((slab, parts, cut, bands), jnp.float32),
        in_specs=[pl.BlockSpec(memory_space=pltpu.SMEM), vmem, vmem],
        out_specs=vmem,
        scratch_shapes=[
            pltpu.VMEM(coeffs.shape, coeffs.dtype),
            pltpu.VMEM(coeffs.shape, coeffs.dtype),
            pltpu.VMEM(coeffs.shape, coeffs.dtype),
            pltpu.VMEM((slab, parts, bands, bands), SENT),
            pltpu.VMEM((n_pw, slab, parts, cut, bands), SENT),
            pltpu.VMEM((parts, bands, bands), jnp.float32),
            pltpu.VMEM((parts, rows, bands), jnp.float32),
            pltpu.SemaphoreType.DMA((slab,)),
            pltpu.SemaphoreType.DMA((slab,)),
            pltpu.SemaphoreType.DMA((slab,)),
            pltpu.SemaphoreType.DMA((slab,)),
            pltpu.SemaphoreType.DMA((slab // GROUP, n_pw)),
            pltpu.SemaphoreType.DMA((slab // GROUP, n_pw)),
        ],
        compiler_params=pltpu.CompilerParams(
            collective_id=0, has_side_effects=True, vmem_limit_bytes=58 * 1024 * 1024),
        cost_estimate=pl.CostEstimate(flops=flops, bytes_accessed=3 * coeffs.size, transcendentals=0),
    )(inverse, gshift[:, None], coeffs)
    return jnp.transpose(jnp.take(summed, local_order, axis=0), (2, 0, 1, 3))


def solution(mesh):
    placed = (P("ka", None, "pw", None), P("ka"), P())
    return jax.shard_map(
        functools.partial(on_device, mesh.shape["ka"], mesh.shape["pw"]), mesh=mesh, in_specs=placed,
        out_specs=P("pw", "ka", None, None), check_vma=False
    )
```

```python
import functools

import jax
import jax.numpy as jnp
from jax import lax
from jax.experimental import pallas as pl
from jax.experimental.pallas import tpu as pltpu
from jax.sharding import PartitionSpec as P

SHIFT_DEV = 2
MESH = pl.DeviceIdType.MESH
SENT = jnp.float32


def contract(a, b):
    return lax.dot_general(a, b, (((0,), (0,)), ((), ())), preferred_element_type=jnp.float32)


def kernel(n_ka, n_pw, inv_ref, gshift_ref, x_ref, out_ref, y, own_k, sorted_own, sent, got, part, moved,
           y_send, y_recv, k_send, k_recv, p_send, p_recv):
    slab, _, rows, bands = x_ref.shape
    per_pw = slab // n_pw
    cut = bands // n_pw
    ka, pw = lax.axis_index("ka"), lax.axis_index("pw")
    source = lax.rem(ka + SHIFT_DEV, n_ka)
    target = lax.rem(ka + n_ka - SHIFT_DEV, n_ka)
    wrapped = ka >= n_ka - SHIFT_DEV
    relay = n_ka - SHIFT_DEV - 1
    feeds_wrapped = ka == 0
    feeds_relay = ka == 1
    is_relay = ka == relay

    def peer(d):
        return lax.rem(pw + d, n_pw)

    barrier = pltpu.get_barrier_semaphore()

    @pl.loop(1, n_pw)
    def _(d):
        pl.semaphore_signal(barrier, inc=1, device_id=(ka, peer(d)), device_id_type=MESH)

    def greet(other_ka, other_pw):
        pl.semaphore_signal(barrier, inc=1, device_id=(other_ka, other_pw), device_id_type=MESH)

    @pl.when(ka == n_ka - 2)
    def _():
        @pl.loop(0, n_pw)
        def _(d):
            greet(0, peer(d))

    @pl.when(ka == n_ka - 1)
    def _():
        @pl.loop(0, n_pw)
        def _(d):
            greet(relay, peer(d))

    @pl.when(jnp.logical_not(wrapped))
    def _():
        greet(source, pw)

    @pl.when(is_relay)
    def _():
        greet(1, pw)
        pl.semaphore_wait(barrier, 2 * n_pw)

    @pl.when(feeds_wrapped)
    def _():
        pl.semaphore_wait(barrier, 2 * n_pw - 1)

    @pl.when(jnp.logical_not(jnp.logical_or(feeds_wrapped, is_relay)))
    def _():
        pl.semaphore_wait(barrier, n_pw)

    def shift_plain(k):
        return pltpu.make_async_remote_copy(
            src_ref=x_ref.at[k], dst_ref=y.at[k], send_sem=y_send.at[k], recv_sem=y_recv.at[k],
            device_id=(target, pw), device_id_type=MESH)

    def shift_to_wrapped(kk, d):
        k = peer(d) * per_pw + kk
        slot = pw * per_pw + kk
        return pltpu.make_async_remote_copy(
            src_ref=x_ref.at[k], dst_ref=y.at[slot], send_sem=y_send.at[k], recv_sem=y_recv.at[slot],
            device_id=(target, peer(d)), device_id_type=MESH)

    def own_to_peer(kk, d):
        k = peer(d) * per_pw + kk
        slot = pw * per_pw + kk
        return pltpu.make_async_remote_copy(
            src_ref=sorted_own.at[k], dst_ref=own_k.at[slot], send_sem=k_send.at[k], recv_sem=k_recv.at[slot],
            device_id=(ka, peer(d)), device_id_type=MESH)

    def shift_to_relay(k):
        return pltpu.make_async_remote_copy(
            src_ref=x_ref.at[k], dst_ref=own_k.at[k], send_sem=y_send.at[k], recv_sem=k_recv.at[k],
            device_id=(relay, pw), device_id_type=MESH)

    def relay_onward(kk, d):
        k = peer(d) * per_pw + kk
        slot = pw * per_pw + kk
        return pltpu.make_async_remote_copy(
            src_ref=own_k.at[k], dst_ref=y.at[slot], send_sem=k_send.at[k], recv_sem=y_recv.at[slot],
            device_id=(n_ka - 1, peer(d)), device_id_type=MESH)

    def piece(j):
        return pl.ds(pl.multiple_of(j * cut, cut), cut)

    def sum_onward(k, j, slot, to):
        return pltpu.make_async_remote_copy(
            src_ref=sent.at[k, :, piece(j), :], dst_ref=got.at[slot, k],
            send_sem=p_send.at[k, j], recv_sem=p_recv.at[k, slot],
            device_id=(ka, to), device_id_type=MESH)

    right, left = lax.rem(pw + 1, n_pw), lax.rem(pw + n_pw - 1, n_pw)

    def send_right(k, j):
        sum_onward(k, j, j, right).start()

    def send_left(k, j):
        @pl.when(j == pw - 1)
        def _():
            sum_onward(k, j, n_pw, left).start()

        @pl.when(j < pw - 1)
        def _():
            sum_onward(k, j, j, left).start()

    def add_arrived(k, j):
        sum_onward(k, j, j, right).wait_recv()
        sent[k, :, piece(j), :] = sent[k, :, piece(j), :] + got[j, k]

    def whole_to_peer(kk, d):
        k = pw * per_pw + kk
        return pltpu.make_async_remote_copy(
            src_ref=sent.at[k, :, pl.ds(pl.multiple_of(peer(d) * cut, cut), cut), :],
            dst_ref=got.at[pw, k],
            send_sem=p_send.at[kk, peer(d)], recv_sem=p_recv.at[kk, pw],
            device_id=(ka, peer(d)), device_id_type=MESH)

    def whole_from_peer(kk, d):
        k = peer(d) * per_pw + kk
        return pltpu.make_async_remote_copy(
            src_ref=sent.at[k, :, pl.ds(pl.multiple_of(peer(d) * cut, cut), cut), :],
            dst_ref=got.at[peer(d), k],
            send_sem=p_send.at[kk, peer(d)], recv_sem=p_recv.at[kk, peer(d)],
            device_id=(ka, peer(d)), device_id_type=MESH)

    @pl.when(feeds_wrapped)
    def _():
        @pl.loop(0, per_pw)
        def _(kk):
            @pl.loop(0, n_pw)
            def _(d):
                shift_to_wrapped(kk, d).start()

    @pl.when(feeds_relay)
    def _():
        @pl.loop(0, per_pw)
        def _(kk):
            @pl.loop(0, n_pw)
            def _(d):
                shift_to_relay(peer(d) * per_pw + kk).start()

    @pl.when(ka >= 2)
    def _():
        @pl.loop(0, slab)
        def _(k):
            shift_plain(k).start()

    def keep(k):
        sent[k] = part[...].astype(SENT)
        out_ref[k] = part[:, pl.ds(pl.multiple_of(pw * cut, cut), cut), :]

    @pl.when(jnp.logical_not(wrapped))
    def _():
        @pl.loop(0, slab + 1)
        def _(step):
            @pl.when(step < slab)
            def _():
                k = step

                @pl.when(is_relay)
                def _():
                    kk, d = k // n_pw, lax.rem(k, n_pw)
                    shift_to_relay(peer(d) * per_pw + kk).wait_recv()
                    relay_onward(kk, d).start()

                shift_plain(k).wait_recv()
                mine = x_ref[inv_ref[k]]
                other = y[k]
                part[0] = contract(mine.reshape(2 * rows, bands), other.reshape(2 * rows, bands))
                part[1] = contract(mine[0], other[1]) - contract(mine[1], other[0])
                keep(k)

                @pl.when(pw == 0)
                def _():
                    @pl.loop(1, n_pw)
                    def _(i):
                        send_right(k, n_pw - i)

                @pl.when(pw == n_pw - 1)
                def _():
                    @pl.loop(0, n_pw - 1)
                    def _(j):
                        send_left(k, j)

            @pl.when(step > 0)
            def _():
                k = step - 1

                @pl.loop(0, n_pw)
                def _(j):
                    @pl.when(jnp.logical_and(j > pw, pw > 0))
                    def _():
                        add_arrived(k, j)
                        send_right(k, j)

                    @pl.when(jnp.logical_and(j < pw, pw < n_pw - 1))
                    def _():
                        add_arrived(k, j)
                        send_left(k, j)

        @pl.loop(0, slab)
        def _(k):
            @pl.when(pw > 0)
            def _():
                sum_onward(k, pw, pw, right).wait_recv()
                out_ref[k] = out_ref[k] + got[pw, k]

            @pl.when(pw < n_pw - 1)
            def _():
                sum_onward(k, pw, n_pw, left).wait_recv()
                out_ref[k] = out_ref[k] + got[n_pw, k]

        @pl.loop(0, slab)
        def _(k):
            @pl.loop(1, n_pw)
            def _(d):
                sum_onward(k, peer(d), peer(d), right).wait_send()

    @pl.when(is_relay)
    def _():
        @pl.loop(0, per_pw)
        def _(kk):
            @pl.loop(0, n_pw)
            def _(d):
                relay_onward(kk, d).wait_send()

    @pl.when(wrapped)
    def _():
        @pl.loop(0, per_pw)
        def _(kk):
            own_k[pw * per_pw + kk] = x_ref[inv_ref[pw * per_pw + kk]]

            @pl.loop(1, n_pw)
            def _(d):
                k = peer(d) * per_pw + kk
                sorted_own[k] = x_ref[inv_ref[k]]
                own_to_peer(kk, d).start()

        @pl.loop(0, per_pw)
        def _(kk):
            @pl.loop(0, n_pw)
            def _(s):
                slot = s * per_pw + kk
                pltpu.make_async_remote_copy(
                    src_ref=x_ref.at[slot], dst_ref=y.at[slot], send_sem=y_send.at[slot], recv_sem=y_recv.at[slot],
                    device_id=(target, pw), device_id_type=MESH).wait_recv()

            @pl.loop(1, n_pw)
            def _(d):
                slot = peer(d) * per_pw + kk
                pltpu.make_async_remote_copy(
                    src_ref=sorted_own.at[slot], dst_ref=own_k.at[slot], send_sem=k_send.at[slot],
                    recv_sem=k_recv.at[slot], device_id=(ka, peer(d)), device_id_type=MESH).wait_recv()

            part[...] = jnp.zeros_like(part)

            @pl.loop(0, n_pw)
            def _(i):
                wanted = gshift_ref[pl.ds(pl.multiple_of(i * rows, rows), rows), :]
                moved[...] = jnp.zeros_like(moved)

                @pl.loop(0, n_pw)
                def _(s):
                    place = lax.broadcasted_iota(jnp.int32, (rows, rows), 1) + s * rows
                    chosen = jnp.where(place == wanted, 1.0, 0.0).astype(jnp.bfloat16)
                    for c in range(2):
                        moved[c] += jnp.dot(chosen, y[s * per_pw + kk, c], preferred_element_type=jnp.float32)

                mine = own_k[i * per_pw + kk]
                other = moved[...].astype(jnp.bfloat16)
                part[0] += contract(mine.reshape(2 * rows, bands), other.reshape(2 * rows, bands))
                part[1] += contract(mine[0], other[1]) - contract(mine[1], other[0])

            keep(pw * per_pw + kk)

            @pl.loop(1, n_pw)
            def _(d):
                whole_to_peer(kk, d).start()

        @pl.loop(0, per_pw)
        def _(kk):
            @pl.loop(1, n_pw)
            def _(d):
                whole_from_peer(kk, d).wait_recv()
                k = peer(d) * per_pw + kk
                out_ref[k] = got[peer(d), k].astype(jnp.float32)

        @pl.loop(0, per_pw)
        def _(kk):
            @pl.loop(1, n_pw)
            def _(d):
                whole_to_peer(kk, d).wait_send()
                own_to_peer(kk, d).wait_send()

    @pl.when(feeds_wrapped)
    def _():
        @pl.loop(0, per_pw)
        def _(kk):
            @pl.loop(0, n_pw)
            def _(d):
                shift_to_wrapped(kk, d).wait_send()

    @pl.when(feeds_relay)
    def _():
        @pl.loop(0, slab)
        def _(k):
            shift_to_relay(k).wait_send()

    @pl.when(ka >= 2)
    def _():
        @pl.loop(0, slab)
        def _(k):
            shift_plain(k).wait_send()


def on_device(n_ka, n_pw, coeffs, neighbour, gshift):
    slab, parts, rows, bands = coeffs.shape
    cut = bands // n_pw
    points = jnp.arange(slab, dtype=jnp.int32)
    local_order = neighbour % slab
    inverse = jnp.sum(jnp.where(local_order[:, None] == points[None, :], points[:, None], 0), axis=0)
    vmem = pl.BlockSpec(memory_space=pltpu.VMEM)
    flops = 8 * slab * rows * bands * bands
    summed = pl.pallas_call(
        functools.partial(kernel, n_ka, n_pw),
        out_shape=jax.ShapeDtypeStruct((slab, parts, cut, bands), jnp.float32),
        in_specs=[pl.BlockSpec(memory_space=pltpu.SMEM), vmem, vmem],
        out_specs=vmem,
        scratch_shapes=[
            pltpu.VMEM(coeffs.shape, coeffs.dtype),
            pltpu.VMEM(coeffs.shape, coeffs.dtype),
            pltpu.VMEM(coeffs.shape, coeffs.dtype),
            pltpu.VMEM((slab, parts, bands, bands), SENT),
            pltpu.VMEM((n_pw + 1, slab, parts, cut, bands), SENT),
            pltpu.VMEM((parts, bands, bands), jnp.float32),
            pltpu.VMEM((parts, rows, bands), jnp.float32),
            pltpu.SemaphoreType.DMA((slab,)),
            pltpu.SemaphoreType.DMA((slab,)),
            pltpu.SemaphoreType.DMA((slab,)),
            pltpu.SemaphoreType.DMA((slab,)),
            pltpu.SemaphoreType.DMA((slab, n_pw + 1)),
            pltpu.SemaphoreType.DMA((slab, n_pw + 1)),
        ],
        compiler_params=pltpu.CompilerParams(
            collective_id=0, has_side_effects=True, vmem_limit_bytes=58 * 1024 * 1024),
        cost_estimate=pl.CostEstimate(flops=flops, bytes_accessed=3 * coeffs.size, transcendentals=0),
    )(inverse, gshift[:, None], coeffs)
    return jnp.transpose(jnp.take(summed, local_order, axis=0), (2, 0, 1, 3))


def solution(mesh):
    placed = (P("ka", None, "pw", None), P("ka"), P())
    return jax.shard_map(
        functools.partial(on_device, mesh.shape["ka"], mesh.shape["pw"]), mesh=mesh, in_specs=placed,
        out_specs=P("pw", "ka", None, None), check_vma=False
    )
```

```python
import functools

import jax
import jax.numpy as jnp
from jax import lax
from jax.experimental import pallas as pl
from jax.experimental.pallas import tpu as pltpu
from jax.sharding import PartitionSpec as P

SHIFT_DEV = 2
WINDOW = 4
MESH = pl.DeviceIdType.MESH
SENT = jnp.float32


def contract(a, b):
    return lax.dot_general(a, b, (((0,), (0,)), ((), ())), preferred_element_type=jnp.float32)


def kernel(n_ka, n_pw, inv_ref, gshift_ref, x_ref, out_ref, y, own_k, sorted_own, sent, got, part, moved,
           y_send, y_recv, k_send, k_recv, p_send, p_recv):
    slab, _, rows, bands = x_ref.shape
    per_pw = slab // n_pw
    cut = bands // n_pw
    ka, pw = lax.axis_index("ka"), lax.axis_index("pw")
    source = lax.rem(ka + SHIFT_DEV, n_ka)
    target = lax.rem(ka + n_ka - SHIFT_DEV, n_ka)
    wrapped = ka >= n_ka - SHIFT_DEV
    relay = n_ka - SHIFT_DEV - 1
    feeds_wrapped = ka == 0
    feeds_relay = ka == 1
    is_relay = ka == relay

    def peer(d):
        return lax.rem(pw + d, n_pw)

    barrier = pltpu.get_barrier_semaphore()

    @pl.loop(1, n_pw)
    def _(d):
        pl.semaphore_signal(barrier, inc=1, device_id=(ka, peer(d)), device_id_type=MESH)

    def greet(other_ka, other_pw):
        pl.semaphore_signal(barrier, inc=1, device_id=(other_ka, other_pw), device_id_type=MESH)

    @pl.when(ka == n_ka - 2)
    def _():
        @pl.loop(0, n_pw)
        def _(d):
            greet(0, peer(d))

    @pl.when(ka == n_ka - 1)
    def _():
        @pl.loop(0, n_pw)
        def _(d):
            greet(relay, peer(d))

    @pl.when(jnp.logical_not(wrapped))
    def _():
        greet(source, pw)

    @pl.when(is_relay)
    def _():
        greet(1, pw)
        pl.semaphore_wait(barrier, 2 * n_pw)

    @pl.when(feeds_wrapped)
    def _():
        pl.semaphore_wait(barrier, 2 * n_pw - 1)

    @pl.when(jnp.logical_not(jnp.logical_or(feeds_wrapped, is_relay)))
    def _():
        pl.semaphore_wait(barrier, n_pw)

    def shift_plain(k):
        return pltpu.make_async_remote_copy(
            src_ref=x_ref.at[k], dst_ref=y.at[k], send_sem=y_send.at[k], recv_sem=y_recv.at[k],
            device_id=(target, pw), device_id_type=MESH)

    def shift_to_wrapped(kk, d):
        k = peer(d) * per_pw + kk
        slot = pw * per_pw + kk
        return pltpu.make_async_remote_copy(
            src_ref=x_ref.at[k], dst_ref=y.at[slot], send_sem=y_send.at[k], recv_sem=y_recv.at[slot],
            device_id=(target, peer(d)), device_id_type=MESH)

    def own_to_peer(kk, d):
        k = peer(d) * per_pw + kk
        slot = pw * per_pw + kk
        return pltpu.make_async_remote_copy(
            src_ref=sorted_own.at[k], dst_ref=own_k.at[slot], send_sem=k_send.at[k], recv_sem=k_recv.at[slot],
            device_id=(ka, peer(d)), device_id_type=MESH)

    def shift_to_relay(k):
        return pltpu.make_async_remote_copy(
            src_ref=x_ref.at[k], dst_ref=own_k.at[k], send_sem=y_send.at[k], recv_sem=k_recv.at[k],
            device_id=(relay, pw), device_id_type=MESH)

    def relay_onward(kk, d):
        k = peer(d) * per_pw + kk
        slot = pw * per_pw + kk
        return pltpu.make_async_remote_copy(
            src_ref=own_k.at[k], dst_ref=y.at[slot], send_sem=k_send.at[k], recv_sem=y_recv.at[slot],
            device_id=(n_ka - 1, peer(d)), device_id_type=MESH)

    def piece(j):
        return pl.ds(pl.multiple_of(j * cut, cut), cut)

    def sum_onward(k, j, slot, to):
        return pltpu.make_async_remote_copy(
            src_ref=sent.at[k, :, piece(j), :], dst_ref=got.at[slot, k],
            send_sem=p_send.at[k, j], recv_sem=p_recv.at[k, slot],
            device_id=(ka, to), device_id_type=MESH)

    right, left = lax.rem(pw + 1, n_pw), lax.rem(pw + n_pw - 1, n_pw)

    def send_right(k, j):
        sum_onward(k, j, j, right).start()

    def send_left(k, j):
        @pl.when(j == pw - 1)
        def _():
            sum_onward(k, j, n_pw, left).start()

        @pl.when(j < pw - 1)
        def _():
            sum_onward(k, j, j, left).start()

    def add_arrived(k, j):
        sum_onward(k, j, j, right).wait_recv()
        sent[k, :, piece(j), :] = sent[k, :, piece(j), :] + got[j, k]

    def whole_to_peer(kk, d):
        k = pw * per_pw + kk
        return pltpu.make_async_remote_copy(
            src_ref=sent.at[k, :, pl.ds(pl.multiple_of(peer(d) * cut, cut), cut), :],
            dst_ref=got.at[pw, k],
            send_sem=p_send.at[kk, peer(d)], recv_sem=p_recv.at[kk, pw],
            device_id=(ka, peer(d)), device_id_type=MESH)

    def whole_from_peer(kk, d):
        k = peer(d) * per_pw + kk
        return pltpu.make_async_remote_copy(
            src_ref=sent.at[k, :, pl.ds(pl.multiple_of(peer(d) * cut, cut), cut), :],
            dst_ref=got.at[peer(d), k],
            send_sem=p_send.at[kk, peer(d)], recv_sem=p_recv.at[kk, peer(d)],
            device_id=(ka, peer(d)), device_id_type=MESH)

    def launch(t):
        kk, d = t // n_pw, lax.rem(t, n_pw)

        @pl.when(feeds_wrapped)
        def _():
            shift_to_wrapped(kk, d).start()

        @pl.when(feeds_relay)
        def _():
            shift_to_relay(peer(d) * per_pw + kk).start()

        @pl.when(ka >= 2)
        def _():
            shift_plain(t).start()

    def keep(k):
        sent[k] = part[...].astype(SENT)
        out_ref[k] = part[:, pl.ds(pl.multiple_of(pw * cut, cut), cut), :]

    @pl.when(jnp.logical_not(wrapped))
    def _():
        @pl.loop(0, WINDOW)
        def _(t):
            launch(t)

        @pl.loop(0, slab + 1)
        def _(step):
            @pl.when(step < slab - WINDOW)
            def _():
                launch(step + WINDOW)

            @pl.when(step < slab)
            def _():
                k = step

                @pl.when(is_relay)
                def _():
                    kk, d = k // n_pw, lax.rem(k, n_pw)
                    shift_to_relay(peer(d) * per_pw + kk).wait_recv()
                    relay_onward(kk, d).start()

                shift_plain(k).wait_recv()
                mine = x_ref[inv_ref[k]]
                other = y[k]
                part[0] = contract(mine.reshape(2 * rows, bands), other.reshape(2 * rows, bands))
                part[1] = contract(mine[0], other[1]) - contract(mine[1], other[0])
                keep(k)

                @pl.when(pw == 0)
                def _():
                    @pl.loop(1, n_pw)
                    def _(i):
                        send_right(k, n_pw - i)

                @pl.when(pw == n_pw - 1)
                def _():
                    @pl.loop(0, n_pw - 1)
                    def _(j):
                        send_left(k, j)

            @pl.when(step > 0)
            def _():
                k = step - 1

                @pl.loop(0, n_pw)
                def _(j):
                    @pl.when(jnp.logical_and(j > pw, pw > 0))
                    def _():
                        add_arrived(k, j)
                        send_right(k, j)

                    @pl.when(jnp.logical_and(j < pw, pw < n_pw - 1))
                    def _():
                        add_arrived(k, j)
                        send_left(k, j)

        @pl.loop(0, slab)
        def _(k):
            @pl.when(pw > 0)
            def _():
                sum_onward(k, pw, pw, right).wait_recv()
                out_ref[k] = out_ref[k] + got[pw, k]

            @pl.when(pw < n_pw - 1)
            def _():
                sum_onward(k, pw, n_pw, left).wait_recv()
                out_ref[k] = out_ref[k] + got[n_pw, k]

        @pl.loop(0, slab)
        def _(k):
            @pl.loop(1, n_pw)
            def _(d):
                sum_onward(k, peer(d), peer(d), right).wait_send()

    @pl.when(is_relay)
    def _():
        @pl.loop(0, per_pw)
        def _(kk):
            @pl.loop(0, n_pw)
            def _(d):
                relay_onward(kk, d).wait_send()

    @pl.when(wrapped)
    def _():
        @pl.loop(0, n_pw)
        def _(t):
            shift_plain(t).start()

        @pl.loop(0, per_pw)
        def _(kk):
            own_k[pw * per_pw + kk] = x_ref[inv_ref[pw * per_pw + kk]]

            @pl.loop(1, n_pw)
            def _(d):
                k = peer(d) * per_pw + kk
                sorted_own[k] = x_ref[inv_ref[k]]
                own_to_peer(kk, d).start()

        @pl.loop(0, per_pw)
        def _(kk):
            @pl.when(kk < per_pw - 1)
            def _():
                @pl.loop(0, n_pw)
                def _(t):
                    shift_plain((kk + 1) * n_pw + t).start()

            @pl.loop(0, n_pw)
            def _(s):
                slot = s * per_pw + kk
                pltpu.make_async_remote_copy(
                    src_ref=x_ref.at[slot], dst_ref=y.at[slot], send_sem=y_send.at[slot], recv_sem=y_recv.at[slot],
                    device_id=(target, pw), device_id_type=MESH).wait_recv()

            @pl.loop(1, n_pw)
            def _(d):
                slot = peer(d) * per_pw + kk
                pltpu.make_async_remote_copy(
                    src_ref=sorted_own.at[slot], dst_ref=own_k.at[slot], send_sem=k_send.at[slot],
                    recv_sem=k_recv.at[slot], device_id=(ka, peer(d)), device_id_type=MESH).wait_recv()

            part[...] = jnp.zeros_like(part)

            @pl.loop(0, n_pw)
            def _(i):
                wanted = gshift_ref[pl.ds(pl.multiple_of(i * rows, rows), rows), :]
                moved[...] = jnp.zeros_like(moved)

                @pl.loop(0, n_pw)
                def _(s):
                    place = lax.broadcasted_iota(jnp.int32, (rows, rows), 1) + s * rows
                    chosen = jnp.where(place == wanted, 1.0, 0.0).astype(jnp.bfloat16)
                    for c in range(2):
                        moved[c] += jnp.dot(chosen, y[s * per_pw + kk, c], preferred_element_type=jnp.float32)

                mine = own_k[i * per_pw + kk]
                other = moved[...].astype(jnp.bfloat16)
                part[0] += contract(mine.reshape(2 * rows, bands), other.reshape(2 * rows, bands))
                part[1] += contract(mine[0], other[1]) - contract(mine[1], other[0])

            keep(pw * per_pw + kk)

            @pl.loop(1, n_pw)
            def _(d):
                whole_to_peer(kk, d).start()

        @pl.loop(0, per_pw)
        def _(kk):
            @pl.loop(1, n_pw)
            def _(d):
                whole_from_peer(kk, d).wait_recv()
                k = peer(d) * per_pw + kk
                out_ref[k] = got[peer(d), k].astype(jnp.float32)

        @pl.loop(0, per_pw)
        def _(kk):
            @pl.loop(1, n_pw)
            def _(d):
                whole_to_peer(kk, d).wait_send()
                own_to_peer(kk, d).wait_send()

    @pl.when(feeds_wrapped)
    def _():
        @pl.loop(0, per_pw)
        def _(kk):
            @pl.loop(0, n_pw)
            def _(d):
                shift_to_wrapped(kk, d).wait_send()

    @pl.when(feeds_relay)
    def _():
        @pl.loop(0, slab)
        def _(k):
            shift_to_relay(k).wait_send()

    @pl.when(ka >= 2)
    def _():
        @pl.loop(0, slab)
        def _(k):
            shift_plain(k).wait_send()


def on_device(n_ka, n_pw, coeffs, neighbour, gshift):
    slab, parts, rows, bands = coeffs.shape
    cut = bands // n_pw
    points = jnp.arange(slab, dtype=jnp.int32)
    local_order = neighbour % slab
    inverse = jnp.sum(jnp.where(local_order[:, None] == points[None, :], points[:, None], 0), axis=0)
    vmem = pl.BlockSpec(memory_space=pltpu.VMEM)
    flops = 8 * slab * rows * bands * bands
    summed = pl.pallas_call(
        functools.partial(kernel, n_ka, n_pw),
        out_shape=jax.ShapeDtypeStruct((slab, parts, cut, bands), jnp.float32),
        in_specs=[pl.BlockSpec(memory_space=pltpu.SMEM), vmem, vmem],
        out_specs=vmem,
        scratch_shapes=[
            pltpu.VMEM(coeffs.shape, coeffs.dtype),
            pltpu.VMEM(coeffs.shape, coeffs.dtype),
            pltpu.VMEM(coeffs.shape, coeffs.dtype),
            pltpu.VMEM((slab, parts, bands, bands), SENT),
            pltpu.VMEM((n_pw + 1, slab, parts, cut, bands), SENT),
            pltpu.VMEM((parts, bands, bands), jnp.float32),
            pltpu.VMEM((parts, rows, bands), jnp.float32),
            pltpu.SemaphoreType.DMA((slab,)),
            pltpu.SemaphoreType.DMA((slab,)),
            pltpu.SemaphoreType.DMA((slab,)),
            pltpu.SemaphoreType.DMA((slab,)),
            pltpu.SemaphoreType.DMA((slab, n_pw + 1)),
            pltpu.SemaphoreType.DMA((slab, n_pw + 1)),
        ],
        compiler_params=pltpu.CompilerParams(
            collective_id=0, has_side_effects=True, vmem_limit_bytes=58 * 1024 * 1024),
        cost_estimate=pl.CostEstimate(flops=flops, bytes_accessed=3 * coeffs.size, transcendentals=0),
    )(inverse, gshift[:, None], coeffs)
    return jnp.transpose(jnp.take(summed, local_order, axis=0), (2, 0, 1, 3))


def solution(mesh):
    placed = (P("ka", None, "pw", None), P("ka"), P())
    return jax.shard_map(
        functools.partial(on_device, mesh.shape["ka"], mesh.shape["pw"]), mesh=mesh, in_specs=placed,
        out_specs=P("pw", "ka", None, None), check_vma=False
    )
```

```python
import functools

import jax
import jax.numpy as jnp
from jax import lax
from jax.experimental import pallas as pl
from jax.experimental.pallas import tpu as pltpu
from jax.sharding import PartitionSpec as P

SHIFT_DEV = 2
WINDOW = 2
MESH = pl.DeviceIdType.MESH
SENT = jnp.float32


def contract(a, b):
    return lax.dot_general(a, b, (((0,), (0,)), ((), ())), preferred_element_type=jnp.float32)


def kernel(n_ka, n_pw, inv_ref, gshift_ref, x_ref, out_ref, y, own_k, sorted_own, sent, got, part, moved,
           y_send, y_recv, k_send, k_recv, p_send, p_recv):
    slab, _, rows, bands = x_ref.shape
    per_pw = slab // n_pw
    cut = bands // n_pw
    ka, pw = lax.axis_index("ka"), lax.axis_index("pw")
    source = lax.rem(ka + SHIFT_DEV, n_ka)
    target = lax.rem(ka + n_ka - SHIFT_DEV, n_ka)
    wrapped = ka >= n_ka - SHIFT_DEV
    relay = n_ka - SHIFT_DEV - 1
    feeds_wrapped = ka == 0
    feeds_relay = ka == 1
    is_relay = ka == relay

    def peer(d):
        return lax.rem(pw + d, n_pw)

    barrier = pltpu.get_barrier_semaphore()

    @pl.loop(1, n_pw)
    def _(d):
        pl.semaphore_signal(barrier, inc=1, device_id=(ka, peer(d)), device_id_type=MESH)

    def greet(other_ka, other_pw):
        pl.semaphore_signal(barrier, inc=1, device_id=(other_ka, other_pw), device_id_type=MESH)

    @pl.when(ka == n_ka - 2)
    def _():
        @pl.loop(0, n_pw)
        def _(d):
            greet(0, peer(d))

    @pl.when(ka == n_ka - 1)
    def _():
        @pl.loop(0, n_pw)
        def _(d):
            greet(relay, peer(d))

    @pl.when(jnp.logical_not(wrapped))
    def _():
        greet(source, pw)

    @pl.when(is_relay)
    def _():
        greet(1, pw)
        pl.semaphore_wait(barrier, 2 * n_pw)

    @pl.when(feeds_wrapped)
    def _():
        pl.semaphore_wait(barrier, 2 * n_pw - 1)

    @pl.when(jnp.logical_not(jnp.logical_or(feeds_wrapped, is_relay)))
    def _():
        pl.semaphore_wait(barrier, n_pw)

    def shift_plain(k):
        return pltpu.make_async_remote_copy(
            src_ref=x_ref.at[k], dst_ref=y.at[k], send_sem=y_send.at[k], recv_sem=y_recv.at[k],
            device_id=(target, pw), device_id_type=MESH)

    def shift_to_wrapped(kk, d):
        k = peer(d) * per_pw + kk
        slot = pw * per_pw + kk
        return pltpu.make_async_remote_copy(
            src_ref=x_ref.at[k], dst_ref=y.at[slot], send_sem=y_send.at[k], recv_sem=y_recv.at[slot],
            device_id=(target, peer(d)), device_id_type=MESH)

    def own_to_peer(kk, d):
        k = peer(d) * per_pw + kk
        slot = pw * per_pw + kk
        return pltpu.make_async_remote_copy(
            src_ref=sorted_own.at[k], dst_ref=own_k.at[slot], send_sem=k_send.at[k], recv_sem=k_recv.at[slot],
            device_id=(ka, peer(d)), device_id_type=MESH)

    def shift_to_relay(k):
        return pltpu.make_async_remote_copy(
            src_ref=x_ref.at[k], dst_ref=own_k.at[k], send_sem=y_send.at[k], recv_sem=k_recv.at[k],
            device_id=(relay, pw), device_id_type=MESH)

    def relay_onward(kk, d):
        k = peer(d) * per_pw + kk
        slot = pw * per_pw + kk
        return pltpu.make_async_remote_copy(
            src_ref=own_k.at[k], dst_ref=y.at[slot], send_sem=k_send.at[k], recv_sem=y_recv.at[slot],
            device_id=(n_ka - 1, peer(d)), device_id_type=MESH)

    def piece(j):
        return pl.ds(pl.multiple_of(j * cut, cut), cut)

    def sum_onward(k, j, slot, to):
        return pltpu.make_async_remote_copy(
            src_ref=sent.at[k, :, piece(j), :], dst_ref=got.at[slot, k],
            send_sem=p_send.at[k, j], recv_sem=p_recv.at[k, slot],
            device_id=(ka, to), device_id_type=MESH)

    right, left = lax.rem(pw + 1, n_pw), lax.rem(pw + n_pw - 1, n_pw)

    def send_right(k, j):
        sum_onward(k, j, j, right).start()

    def send_left(k, j):
        @pl.when(j == pw - 1)
        def _():
            sum_onward(k, j, n_pw, left).start()

        @pl.when(j < pw - 1)
        def _():
            sum_onward(k, j, j, left).start()

    def add_arrived(k, j):
        sum_onward(k, j, j, right).wait_recv()
        sent[k, :, piece(j), :] = sent[k, :, piece(j), :] + got[j, k]

    def whole_to_peer(kk, d):
        k = pw * per_pw + kk
        return pltpu.make_async_remote_copy(
            src_ref=sent.at[k, :, pl.ds(pl.multiple_of(peer(d) * cut, cut), cut), :],
            dst_ref=got.at[pw, k],
            send_sem=p_send.at[kk, peer(d)], recv_sem=p_recv.at[kk, pw],
            device_id=(ka, peer(d)), device_id_type=MESH)

    def whole_from_peer(kk, d):
        k = peer(d) * per_pw + kk
        return pltpu.make_async_remote_copy(
            src_ref=sent.at[k, :, pl.ds(pl.multiple_of(peer(d) * cut, cut), cut), :],
            dst_ref=got.at[peer(d), k],
            send_sem=p_send.at[kk, peer(d)], recv_sem=p_recv.at[kk, peer(d)],
            device_id=(ka, peer(d)), device_id_type=MESH)

    def launch(t):
        kk, d = t // n_pw, lax.rem(t, n_pw)

        @pl.when(feeds_wrapped)
        def _():
            shift_to_wrapped(kk, d).start()

        @pl.when(feeds_relay)
        def _():
            shift_to_relay(peer(d) * per_pw + kk).start()

        @pl.when(ka >= 2)
        def _():
            shift_plain(t).start()

    def keep(k):
        sent[k] = part[...].astype(SENT)
        out_ref[k] = part[:, pl.ds(pl.multiple_of(pw * cut, cut), cut), :]

    @pl.when(jnp.logical_not(wrapped))
    def _():
        @pl.loop(0, slab)
        def _(t):
            @pl.when(jnp.logical_or(ka > 0, t < WINDOW))
            def _():
                launch(t)

        @pl.loop(0, slab + 1)
        def _(step):
            @pl.when(jnp.logical_and(ka == 0, step < slab - WINDOW))
            def _():
                launch(step + WINDOW)

            @pl.when(step < slab)
            def _():
                k = step

                @pl.when(is_relay)
                def _():
                    kk, d = k // n_pw, lax.rem(k, n_pw)
                    shift_to_relay(peer(d) * per_pw + kk).wait_recv()
                    relay_onward(kk, d).start()

                shift_plain(k).wait_recv()
                mine = x_ref[inv_ref[k]]
                other = y[k]
                part[0] = contract(mine.reshape(2 * rows, bands), other.reshape(2 * rows, bands))
                part[1] = contract(mine[0], other[1]) - contract(mine[1], other[0])
                keep(k)

                @pl.when(pw == 0)
                def _():
                    @pl.loop(1, n_pw)
                    def _(i):
                        send_right(k, n_pw - i)

                @pl.when(pw == n_pw - 1)
                def _():
                    @pl.loop(0, n_pw - 1)
                    def _(j):
                        send_left(k, j)

            @pl.when(step > 0)
            def _():
                k = step - 1

                @pl.loop(0, n_pw)
                def _(j):
                    @pl.when(jnp.logical_and(j > pw, pw > 0))
                    def _():
                        add_arrived(k, j)
                        send_right(k, j)

                    @pl.when(jnp.logical_and(j < pw, pw < n_pw - 1))
                    def _():
                        add_arrived(k, j)
                        send_left(k, j)

        @pl.loop(0, slab)
        def _(k):
            @pl.when(pw > 0)
            def _():
                sum_onward(k, pw, pw, right).wait_recv()
                out_ref[k] = out_ref[k] + got[pw, k]

            @pl.when(pw < n_pw - 1)
            def _():
                sum_onward(k, pw, n_pw, left).wait_recv()
                out_ref[k] = out_ref[k] + got[n_pw, k]

        @pl.loop(0, slab)
        def _(k):
            @pl.loop(1, n_pw)
            def _(d):
                sum_onward(k, peer(d), peer(d), right).wait_send()

    @pl.when(is_relay)
    def _():
        @pl.loop(0, per_pw)
        def _(kk):
            @pl.loop(0, n_pw)
            def _(d):
                relay_onward(kk, d).wait_send()

    @pl.when(wrapped)
    def _():
        @pl.loop(0, slab)
        def _(t):
            shift_plain(t).start()

        @pl.loop(0, per_pw)
        def _(kk):
            own_k[pw * per_pw + kk] = x_ref[inv_ref[pw * per_pw + kk]]

            @pl.loop(1, n_pw)
            def _(d):
                k = peer(d) * per_pw + kk
                sorted_own[k] = x_ref[inv_ref[k]]
                own_to_peer(kk, d).start()

        @pl.loop(0, per_pw)
        def _(kk):
            @pl.loop(0, n_pw)
            def _(s):
                slot = s * per_pw + kk
                pltpu.make_async_remote_copy(
                    src_ref=x_ref.at[slot], dst_ref=y.at[slot], send_sem=y_send.at[slot], recv_sem=y_recv.at[slot],
                    device_id=(target, pw), device_id_type=MESH).wait_recv()

            @pl.loop(1, n_pw)
            def _(d):
                slot = peer(d) * per_pw + kk
                pltpu.make_async_remote_copy(
                    src_ref=sorted_own.at[slot], dst_ref=own_k.at[slot], send_sem=k_send.at[slot],
                    recv_sem=k_recv.at[slot], device_id=(ka, peer(d)), device_id_type=MESH).wait_recv()

            part[...] = jnp.zeros_like(part)

            @pl.loop(0, n_pw)
            def _(i):
                wanted = gshift_ref[pl.ds(pl.multiple_of(i * rows, rows), rows), :]
                moved[...] = jnp.zeros_like(moved)

                @pl.loop(0, n_pw)
                def _(s):
                    place = lax.broadcasted_iota(jnp.int32, (rows, rows), 1) + s * rows
                    chosen = jnp.where(place == wanted, 1.0, 0.0).astype(jnp.bfloat16)
                    for c in range(2):
                        moved[c] += jnp.dot(chosen, y[s * per_pw + kk, c], preferred_element_type=jnp.float32)

                mine = own_k[i * per_pw + kk]
                other = moved[...].astype(jnp.bfloat16)
                part[0] += contract(mine.reshape(2 * rows, bands), other.reshape(2 * rows, bands))
                part[1] += contract(mine[0], other[1]) - contract(mine[1], other[0])

            keep(pw * per_pw + kk)

            @pl.loop(1, n_pw)
            def _(d):
                whole_to_peer(kk, d).start()

        @pl.loop(0, per_pw)
        def _(kk):
            @pl.loop(1, n_pw)
            def _(d):
                whole_from_peer(kk, d).wait_recv()
                k = peer(d) * per_pw + kk
                out_ref[k] = got[peer(d), k].astype(jnp.float32)

        @pl.loop(0, per_pw)
        def _(kk):
            @pl.loop(1, n_pw)
            def _(d):
                whole_to_peer(kk, d).wait_send()
                own_to_peer(kk, d).wait_send()

    @pl.when(feeds_wrapped)
    def _():
        @pl.loop(0, per_pw)
        def _(kk):
            @pl.loop(0, n_pw)
            def _(d):
                shift_to_wrapped(kk, d).wait_send()

    @pl.when(feeds_relay)
    def _():
        @pl.loop(0, slab)
        def _(k):
            shift_to_relay(k).wait_send()

    @pl.when(ka >= 2)
    def _():
        @pl.loop(0, slab)
        def _(k):
            shift_plain(k).wait_send()


def on_device(n_ka, n_pw, coeffs, neighbour, gshift):
    slab, parts, rows, bands = coeffs.shape
    cut = bands // n_pw
    points = jnp.arange(slab, dtype=jnp.int32)
    local_order = neighbour % slab
    inverse = jnp.sum(jnp.where(local_order[:, None] == points[None, :], points[:, None], 0), axis=0)
    vmem = pl.BlockSpec(memory_space=pltpu.VMEM)
    flops = 8 * slab * rows * bands * bands
    summed = pl.pallas_call(
        functools.partial(kernel, n_ka, n_pw),
        out_shape=jax.ShapeDtypeStruct((slab, parts, cut, bands), jnp.float32),
        in_specs=[pl.BlockSpec(memory_space=pltpu.SMEM), vmem, vmem],
        out_specs=vmem,
        scratch_shapes=[
            pltpu.VMEM(coeffs.shape, coeffs.dtype),
            pltpu.VMEM(coeffs.shape, coeffs.dtype),
            pltpu.VMEM(coeffs.shape, coeffs.dtype),
            pltpu.VMEM((slab, parts, bands, bands), SENT),
            pltpu.VMEM((n_pw + 1, slab, parts, cut, bands), SENT),
            pltpu.VMEM((parts, bands, bands), jnp.float32),
            pltpu.VMEM((parts, rows, bands), jnp.float32),
            pltpu.SemaphoreType.DMA((slab,)),
            pltpu.SemaphoreType.DMA((slab,)),
            pltpu.SemaphoreType.DMA((slab,)),
            pltpu.SemaphoreType.DMA((slab,)),
            pltpu.SemaphoreType.DMA((slab, n_pw + 1)),
            pltpu.SemaphoreType.DMA((slab, n_pw + 1)),
        ],
        compiler_params=pltpu.CompilerParams(
            collective_id=0, has_side_effects=True, vmem_limit_bytes=58 * 1024 * 1024),
        cost_estimate=pl.CostEstimate(flops=flops, bytes_accessed=3 * coeffs.size, transcendentals=0),
    )(inverse, gshift[:, None], coeffs)
    return jnp.transpose(jnp.take(summed, local_order, axis=0), (2, 0, 1, 3))


def solution(mesh):
    placed = (P("ka", None, "pw", None), P("ka"), P())
    return jax.shard_map(
        functools.partial(on_device, mesh.shape["ka"], mesh.shape["pw"]), mesh=mesh, in_specs=placed,
        out_specs=P("pw", "ka", None, None), check_vma=False
    )
```
